256 devices in a mesh: ia: 8 (over z_hi, x), ja: 32 (over y, z_lo, core).
Axes of the slice: x: 4, y: 4, z: 8 (z_hi: 2, z_lo: 4; z = z_hi * 4 + z_lo), core: 2. Of those that a mesh axis runs over, the one named last changes fastest.
Arguments:
- amplitudes: float32 [64, 64, 8192], P('ia', 'ja'), may hold values from -6 to 6
- residual_in: float32 [64, 64, 8192], P('ia', 'ja'), may hold values from -6 to 6
- ladder_ints: float32 [8192, 8192], P('ja'), may hold values from -0.0625 to 0.0625
- occ_energy: float32 [64], replicated, may hold values from -3 to -0.5
- virt_energy: float32 [256], replicated, may hold values from 0.3 to 3
- virt_order: int32 [256], replicated, may hold values from 0 to 255, each once
Outputs:
- residual: float32 [64, 64, 8192], P('ia', 'ja')
- new_amplitudes: float32 [64, 64, 8192], P('ia', 'ja')
The draws below stay inside these ranges and needn't reach their ends.
Inputs may be any that keep to these rules, and one draw needn't show every extreme that they name: `virt_order`: each orbital number appears once; entries h * 32 to (h + 1) * 32 - 1 are the virtuals of irrep h.
All inputs are finite; a program needn't handle non-finite values.
Results may differ from the reference program's by a relative error of at most 0.000059.
Values sent between devices are 32-bit elements; how exact they have to be, the bound alone decides.
No kernel may reach another device: no remote copies, remote signals or barrier semaphores. Data moves between devices by JAX's collectives and lax.ppermute only.
A program may use at most 128 MiB of HBM per device.

```python
import jax
import jax.numpy as jnp
from jax import lax

NOCC = 64
NV = 256
IRREPS = 8
VH = 32
NP = 8192


def steps_of(stream_key, extent, shards, smallest, high):
    loudness = 1.0
    for axis_at, parts in shards:
        draws = jax.random.uniform(jax.random.fold_in(jax.random.fold_in(stream_key, 6), axis_at), (parts,), jnp.float32, smallest / len(shards), high / len(shards))
        loudness = loudness * jnp.repeat(jnp.exp(draws), extent[axis_at] // parts).reshape((-1,) + (1,) * (len(extent) - 1 - axis_at))
    return loudness


def gaussian(rng, shape, scale, bound, split=(), kind=jnp.bfloat16):
    array = jax.random.normal(rng, shape, jnp.float32) * scale
    if len(split) > 0:
        array = steps_of(rng, shape, split, -0.22, 0.18) * array
    return jnp.clip(array, min=-bound, max=bound).astype(kind)


def setup_inputs(seed: int = 0) -> dict:
    splits = jax.random.split(jax.random.key(seed), 7)
    return {
        "amplitudes": gaussian(splits[0], (NOCC, NOCC, NP), 1.0, 6.0, ((0, 8), (1, 32)), jnp.float32),
        "residual_in": gaussian(splits[1], (NOCC, NOCC, NP), 1.0, 6.0, ((0, 8), (1, 32)), jnp.float32),
        "ladder_ints": gaussian(splits[2], (NP, NP), NP ** -0.5, 0.0625, ((0, 32),), jnp.float32),
        "occ_energy": jnp.clip(jax.random.uniform(splits[3], (NOCC,), jnp.float32, -3.0, -0.5), -3.0, -0.5),
        "virt_energy": jnp.clip(jax.random.uniform(splits[4], (NV,), jnp.float32, 0.3, 3.0), 0.3, 3.0),
        "virt_order": jax.random.permutation(splits[5], NV).astype(jnp.int32),
    }


def reference(amplitudes, residual_in, ladder_ints, occ_energy, virt_energy, virt_order):
    flat = amplitudes.reshape(NOCC * NOCC, NP)
    ladder = jnp.dot(flat, ladder_ints.T, precision=lax.Precision.HIGHEST, preferred_element_type=jnp.float32)
    ladder = ladder.reshape(NOCC, NOCC, NP)
    mirrored = ladder.reshape(NOCC, NOCC, IRREPS, VH, VH).transpose(1, 0, 2, 4, 3).reshape(NOCC, NOCC, NP)
    residual = residual_in + ladder + mirrored
    grouped = virt_energy[virt_order].reshape(IRREPS, VH)
    pair_energy = (grouped[:, :, None] + grouped[:, None, :]).reshape(NP)
    denominator = pair_energy[None, None, :] - occ_energy[:, None, None] - occ_energy[None, :, None]
    return residual, amplitudes + residual / denominator
```

```python
import jax
import jax.numpy as jnp
from jax import lax
from jax.sharding import PartitionSpec as P

NV = 256
IRREPS = 8
VH = 32


def shards(amplitudes, residual_in, ladder_ints, occ_energy, virt_energy, virt_order):
    first_block, second_block, pair_count = amplitudes.shape
    rows = lax.dot_general(
        lax.all_gather(amplitudes, "ja", axis=1, tiled=True),
        ladder_ints,
        (((2,), (1,)), ((), ())),
        precision=lax.Precision.HIGH,
        preferred_element_type=jnp.float32,
    )
    swapped = lax.all_to_all(rows, "ia", split_axis=1, concat_axis=0, tiled=True)
    mirrored = jnp.swapaxes(swapped, 0, 1)
    both = jnp.stack([rows, mirrored])
    both = lax.all_to_all(both, "ja", split_axis=2, concat_axis=3, tiled=True)
    direct, partner = both[0], both[1]
    partner = partner.reshape(first_block, second_block, IRREPS, VH, VH)
    partner = jnp.swapaxes(partner, 3, 4).reshape(first_block, second_block, pair_count)
    residual = residual_in + direct + partner
    onehot = (virt_order[:, None] == jnp.arange(NV, dtype=jnp.int32)[None, :]).astype(jnp.float32)
    grouped = jnp.dot(
        onehot, virt_energy, precision=lax.Precision.HIGHEST, preferred_element_type=jnp.float32
    ).reshape(IRREPS, VH)
    pair_energy = (grouped[:, :, None] + grouped[:, None, :]).reshape(pair_count)
    first_start = lax.axis_index("ia") * first_block
    second_start = lax.axis_index("ja") * second_block
    first_energy = lax.dynamic_slice_in_dim(occ_energy, first_start, first_block)
    second_energy = lax.dynamic_slice_in_dim(occ_energy, second_start, second_block)
    denominator = (
        pair_energy[None, None, :] - first_energy[:, None, None] - second_energy[None, :, None]
    )
    return (residual, amplitudes + residual / denominator)


def solution(mesh):
    placed = (P("ia", "ja", None), P("ia", "ja", None), P("ja", None), P(), P(), P())
    return jax.shard_map(
        shards,
        mesh=mesh,
        in_specs=placed,
        out_specs=(P("ia", "ja", None), P("ia", "ja", None)),
        check_vma=False,
    )
```

```python
import jax
import jax.numpy as jnp
import numpy as np
from jax import lax
from jax.experimental import pallas as pl
from jax.experimental.pallas import tpu as pltpu
from jax.sharding import PartitionSpec as P

NV = 256
IRREPS = 8
VH = 32
NP = 8192
HALF = NP // 2
TILE = 512
ROWS = 256
COLS = 256
BOTH = ("ia", "ja")
F32 = jnp.float32
BF16 = jnp.bfloat16
VMEM_LIMIT = 40 * 1024 * 1024


def device_at(x, y, z, c):
    z = z % 8
    return (z // 4 * 4 + x % 4) * 32 + (y % 4) * 8 + (z % 4) * 2 + c % 2


def moved(dy=0, dz=0, dc=0):
    return [
        (device_at(x, y, z, c), device_at(x, y + dy, z + dz, c + dc))
        for x in range(4)
        for y in range(4)
        for z in range(8)
        for c in range(2)
    ]


def shift(array, dy=0, dz=0, dc=0):
    return lax.ppermute(array, BOTH, moved(dy, dz, dc))


X_GROUPS = [
    [device_at(x, y, z, c) for x in range(4) for c in range(2)] for y in range(4) for z in range(8)
]


def split(value):
    high = value.astype(BF16)
    return high, (value - high.astype(F32)).astype(BF16)


def accumulate(pieces, own, partner, total, step):
    t_high, t_low = split(jnp.concatenate([piece[...] for piece in pieces], axis=0))
    v_high, v_low = split(jnp.concatenate([own[...], partner[...]], axis=0))
    dims = (((1,), (1,)), ((), ()))
    part = lax.dot_general(t_high, v_low, dims, preferred_element_type=F32)
    part += lax.dot_general(t_low, v_high, dims, preferred_element_type=F32)
    part += lax.dot_general(t_high, v_high, dims, preferred_element_type=F32)

    @pl.when(step == 0)
    def _():
        total[...] = part

    @pl.when(step != 0)
    def _():
        total[...] += part


def slot_of(dy, side, dz):
    return dy * 8 + side * 4 + dz


def first_half_kernel(slots, *refs):
    count = len(refs) - 4
    own, partner, out, total = refs[count:]
    step = pl.program_id(0)
    accumulate(refs[:count], own, partner, total, step)

    @pl.when(step == pl.num_programs(0) - 1)
    def _():
        for block, slot in enumerate(slots):
            for v in range(2):
                out[v, slot] = total[block * 8 : block * 8 + 8, v * COLS : (v + 1) * COLS]


def second_half_kernel(slots, place, *refs):
    count = len(refs) - 14
    own, partner, first = refs[count : count + 3]
    direct, crossed = refs[count + 3 : count + 11], refs[count + 11]
    total, sums = refs[count + 12 :]
    step = pl.program_id(0)
    accumulate(refs[:count], own, partner, total, step)

    @pl.when(step == pl.num_programs(0) - 1)
    def _():
        for block, slot in enumerate(slots):
            dy, side, dz = slot // 8, slot // 4 % 2, slot % 4
            for v in range(2):
                value = first[v, slot] + total[block * 8 : block * 8 + 8, v * COLS : (v + 1) * COLS]
                sums[v, slot] = value
                direct[side * 4 + dz][dy, v] = value
        y, z, c = place[1], place[2], place[3]
        for to in range(4):
            for k in range(2):
                for m in range(2):
                    z_low = to % 2 * 2 + m
                    dy = lax.rem(2 * k + to // 2 - y + 4, 4)
                    up = dy * 8 + lax.rem(z - z_low + 4, 4)
                    down = dy * 8 + 4 + lax.rem(z_low - z + 8, 4)
                    for core in range(2):
                        v = lax.rem(c + core, 2)
                        a, b = sums[v, up], sums[v, down]
                        crossed[2 * to, k, m, core] = jnp.concatenate([a[:4], b[:4]], axis=0)
                        crossed[2 * to + 1, k, m, core] = jnp.concatenate([a[4:], b[4:]], axis=0)


def z_pack_kernel(place, came, *outs):
    z = place[2]
    for d in range(8):
        to = lax.rem(z + d, 8)
        k, x_low, side = to // 4, lax.rem(to // 2, 2), lax.rem(to, 2)
        for x_high in range(2):
            for source in range(2):
                at = (2 * x_high + x_low) * 2 + source
                for core in range(2):
                    parts = []
                    for m in range(2):
                        block = came[at, k, m, core]
                        parts.append(jnp.where(side == 0, block[:4], block[4:]))
                    outs[d][x_high, source, core] = jnp.concatenate(parts, axis=0)


def y_pack_kernel(place, *refs):
    came, outs, held = refs[:8], refs[8:12], refs[12]
    for d in range(8):
        held[d] = came[d][...]
    x, y, z = place[0], place[1], place[2]
    side = lax.rem(z, 2)
    for e in range(4):
        to = lax.rem(y + e, 4)
        z_high, x_high = to // 2, lax.rem(to, 2)
        for z_low in range(4):
            froms = []
            for m in range(2):
                low = lax.rem(x, 2) * 2 + m
                up = lax.rem(z_high * 4 + low + lax.rem(z_low - low + 4, 4), 8)
                down = lax.rem(z_high * 4 + low - lax.rem(low - z_low + 4, 4) + 8, 8)
                froms.append(lax.rem(z - jnp.where(side == 0, up, down) + 8, 8))
            for source in range(2):
                for core in range(2):
                    a = held[froms[0], x_high, source, core]
                    b = held[froms[1], x_high, source, core]
                    outs[e][z_low, source, core] = jnp.concatenate([a[:4], b[4:]], axis=0)


def direct_pack_kernel(*refs):
    came, outs = refs[:8], refs[8:]
    for dy in range(4):
        for n in range(8):
            outs[dy][n] = came[n][dy]


def final_kernel(place, *refs):
    direct, mirror = refs[:4], refs[4:8]
    t_ref, r_ref, pair, first, second, turn, residual, updated, moved_ref = refs[8:]
    y, z, c = place[1], place[2], place[3]
    order = (0, 2, 1, 3)
    for e in range(4):
        for z_low in range(4):
            for core in range(2):
                a, b = mirror[e][z_low, 0, core], mirror[e][z_low, 1, core]
                rows = [s[m * 4 + n : m * 4 + n + 1] for m in range(2) for s in (a, b) for n in order]
                column = (z_low % 2 * 2 + core) * COLS
                group = e * 2 + z_low // 2
                moved_ref[group * 16 : group * 16 + 16, column : column + COLS] = jnp.concatenate(rows, axis=0)
    value = moved_ref[...]
    high = value.astype(BF16)
    rest = value - high.astype(F32)
    middle = rest.astype(BF16)
    low = (rest - middle.astype(F32)).astype(BF16)
    dims = (((1,), (0,)), ((), ()))
    turned = lax.dot_general(high, turn[...], dims, preferred_element_type=F32)
    turned += lax.dot_general(middle, turn[...], dims, preferred_element_type=F32)
    turned += lax.dot_general(low, turn[...], dims, preferred_element_type=F32)
    moved_ref[...] = turned
    for e in range(4):
        source = lax.rem(y - e + 4, 4)
        for z_low in range(4):
            up = lax.rem(z_low - z + 8, 4)
            down = 4 + lax.rem(z - z_low + 4, 4)
            for core in range(2):
                v = lax.rem(c + core, 2)
                column = (z_low % 2 * 2 + core) * COLS
                group = e * 2 + z_low // 2
                at = pl.ds(pl.multiple_of(source * 2048 + z_low * 512 + core * COLS, COLS), COLS)
                straight = jnp.concatenate([direct[e][up, v], direct[e][down, v]], axis=0)
                total = r_ref[:, at] + straight + moved_ref[group * 16 : group * 16 + 16, column : column + COLS]
                residual[:, at] = total
                updated[:, at] = t_ref[:, at] + total / (pair[:, at] - first[...] - second[...])


SMEM = pl.BlockSpec(memory_space=pltpu.SMEM)
VMEM = pl.BlockSpec(memory_space=pltpu.VMEM)
PARAMS = pltpu.CompilerParams(vmem_limit_bytes=VMEM_LIMIT)


def shape(*dims):
    return jax.ShapeDtypeStruct(dims, F32)


def tiles(rows, offset):
    return pl.BlockSpec((rows, TILE), lambda k: (0, k + offset))


def shards(amplitudes, residual_in, ladder_ints, occ_energy, virt_energy, virt_order):
    ia, ja = lax.axis_index("ia"), lax.axis_index("ja")
    place = jnp.stack([ia % 4, ja // 8, ia // 4 * 4 + ja // 2 % 4, ja % 2]).astype(jnp.int32)
    own = amplitudes.reshape(16, NP)

    from_below, from_above = shift(own, dy=1), shift(own, dy=-1)
    up, down = [shift(own[:8], dz=1)], [shift(own[8:], dz=-1)]
    up.append(shift(up[-1], dz=1))
    down.append(shift(down[-1], dz=-1))
    far_up, far_down = shift(from_below[:8], dy=1), shift(from_above[8:], dy=-1)
    up.append(shift(up[-1], dz=1))
    down.append(shift(down[-1], dz=-1))
    partner = shift(ladder_ints, dc=1)

    low = [array[:, :HALF] for array in up + down]
    low = jnp.concatenate(low, axis=0)
    low_below, low_above = shift(low, dy=1), shift(low, dy=-1)
    low_far_up, low_far_down = shift(low_below[:24], dy=1), shift(low_above[24:], dy=-1)

    high_up = jnp.concatenate([from_below[:8, HALF:], from_above[:8, HALF:], far_up[:, HALF:]], axis=0)
    high_down = jnp.concatenate([from_below[8:, HALF:], from_above[8:, HALF:], far_down[:, HALF:]], axis=0)
    high_ups, high_downs = [], []
    for _ in range(3):
        high_up, high_down = shift(high_up, dz=1), shift(high_down, dz=-1)
        high_ups.append(high_up)
        high_downs.append(high_down)

    near = [own, from_below, from_above, far_up, far_down] + up + down
    near_slots = [slot_of(dy, side, 0) for dy in (0, 3, 1) for side in range(2)]
    near_slots += [slot_of(2, 0, 0), slot_of(2, 1, 0)]
    near_slots += [slot_of(0, side, dz) for side in range(2) for dz in (1, 2, 3)]
    low_pieces = [low_below, low_above, low_far_up, low_far_down]
    low_slots = [slot_of(dy, side, dz) for dy in (3, 1) for side in range(2) for dz in (1, 2, 3)]
    low_slots += [slot_of(2, side, dz) for side in range(2) for dz in (1, 2, 3)]
    high_pieces = high_ups + high_downs
    high_slots = [slot_of(dy, side, dz) for side in range(2) for dz in (1, 2, 3) for dy in (3, 1, 2)]

    steps = HALF // TILE
    cost = pl.CostEstimate(flops=2 * 3 * ROWS * 2 * COLS * HALF, bytes_accessed=12 << 20, transcendentals=0)
    whole = pl.BlockSpec((2, 32, 8, COLS), lambda k: (0, 0, 0, 0))
    first = pl.pallas_call(
        lambda *refs: first_half_kernel(near_slots + low_slots, *refs),
        grid=(steps,),
        in_specs=[tiles(p.shape[0], 0) for p in near + low_pieces] + [tiles(COLS, 0)] * 2,
        out_specs=whole,
        out_shape=shape(2, 32, 8, COLS),
        scratch_shapes=[pltpu.VMEM((ROWS, 2 * COLS), F32)],
        compiler_params=PARAMS,
        cost_estimate=cost,
        name="first_half",
    )(*near, *low_pieces, ladder_ints, partner)
    sent = pl.BlockSpec((4, 2, 8, COLS), lambda k: (0, 0, 0, 0))
    *direct, crossed = pl.pallas_call(
        lambda place, *refs: second_half_kernel(near_slots + high_slots, place, *refs),
        grid=(steps,),
        in_specs=[SMEM]
        + [tiles(p.shape[0], steps) for p in near]
        + [tiles(p.shape[0], 0) for p in high_pieces]
        + [tiles(COLS, steps)] * 2
        + [whole],
        out_specs=[sent] * 8 + [pl.BlockSpec((8, 2, 2, 2, 8, COLS), lambda k: (0, 0, 0, 0, 0, 0))],
        out_shape=[shape(4, 2, 8, COLS)] * 8 + [shape(8, 2, 2, 2, 8, COLS)],
        scratch_shapes=[pltpu.VMEM((ROWS, 2 * COLS), F32), pltpu.VMEM((2, 32, 8, COLS), F32)],
        compiler_params=PARAMS,
        cost_estimate=cost,
        name="second_half",
    )(place, *near, *high_pieces, ladder_ints, partner, first)

    came = lax.all_to_all(crossed, BOTH, 0, 0, axis_index_groups=X_GROUPS)
    for n in range(8):
        dz = n % 4
        if dz:
            direct[n] = shift(direct[n], dz=-dz if n < 4 else dz)
    z_sent = pl.pallas_call(
        z_pack_kernel,
        in_specs=[SMEM, VMEM],
        out_specs=[VMEM] * 8,
        out_shape=[shape(2, 2, 2, 8, COLS)] * 8,
        compiler_params=PARAMS,
        name="z_pack",
    )(place, came)
    z_came = [z_sent[0]] + [shift(z_sent[d], dz=d) for d in range(1, 8)]
    direct = pl.pallas_call(
        direct_pack_kernel,
        in_specs=[VMEM] * 8,
        out_specs=[VMEM] * 4,
        out_shape=[shape(8, 2, 8, COLS)] * 4,
        compiler_params=PARAMS,
        name="direct_pack",
    )(*direct)
    direct = [direct[0]] + [shift(direct[dy], dy=dy) for dy in range(1, 4)]
    y_sent = pl.pallas_call(
        y_pack_kernel,
        in_specs=[SMEM] + [VMEM] * 8,
        out_specs=[VMEM] * 4,
        out_shape=[shape(4, 2, 2, 8, COLS)] * 4,
        scratch_shapes=[pltpu.VMEM((8, 2, 2, 2, 8, COLS), F32)],
        compiler_params=PARAMS,
        name="y_pack",
    )(place, *z_came)
    mirror = [y_sent[0]] + [shift(y_sent[e], dy=e) for e in range(1, 4)]

    onehot = (virt_order[:, None] == jnp.arange(NV, dtype=jnp.int32)[None, :]).astype(F32)
    grouped = jnp.dot(
        onehot, virt_energy, precision=lax.Precision.HIGHEST, preferred_element_type=F32
    ).reshape(IRREPS, VH)
    pair_energy = (grouped[:, :, None] + grouped[:, None, :]).reshape(1, NP)
    first_energy = jnp.repeat(lax.dynamic_slice_in_dim(occ_energy, ia * 8, 8), 2).reshape(16, 1)
    second_energy = jnp.tile(lax.dynamic_slice_in_dim(occ_energy, ja * 2, 2), 8).reshape(16, 1)
    spot = jnp.arange(VH * VH, dtype=jnp.int32)
    turn = (spot[None, :] == (spot % VH * VH + spot // VH)[:, None]).astype(BF16)
    residual, updated = pl.pallas_call(
        final_kernel,
        in_specs=[SMEM] + [VMEM] * 14,
        out_specs=[VMEM] * 2,
        out_shape=[shape(16, NP)] * 2,
        scratch_shapes=[pltpu.VMEM((128, VH * VH), F32)],
        compiler_params=PARAMS,
        name="final",
    )(
        place, *direct, *mirror, own, residual_in.reshape(16, NP), pair_energy, first_energy, second_energy, turn
    )
    return residual.reshape(8, 2, NP), updated.reshape(8, 2, NP)


def solution(mesh):
    placed = (P("ia", "ja", None), P("ia", "ja", None), P("ja", None), P(), P(), P())
    return jax.shard_map(
        shards,
        mesh=mesh,
        in_specs=placed,
        out_specs=(P("ia", "ja", None), P("ia", "ja", None)),
        check_vma=False,
    )
```

```python
import jax
import jax.numpy as jnp
from jax import lax
from jax.experimental import pallas as pl
from jax.experimental.pallas import tpu as pltpu
from jax.sharding import PartitionSpec as P

NV = 256
IRREPS = 8
VH = 32
NP = 8192
HALF = NP // 2
TILE = 1024
ROWS = 256
COLS = 256
BOTH = ("ia", "ja")
F32 = jnp.float32
BF16 = jnp.bfloat16
MULTIPLY_LIMIT = 12


def device_at(x, y, z, c):
    z = z % 8
    return (z // 4 * 4 + x % 4) * 32 + (y % 4) * 8 + (z % 4) * 2 + c % 2


def moved(dx=0, dy=0, dz=0, dc=0):
    return [
        (device_at(x, y, z, c), device_at(x + dx, y + dy, z + dz, c + dc))
        for x in range(4)
        for y in range(4)
        for z in range(8)
        for c in range(2)
    ]


def shift(array, **steps):
    return lax.ppermute(array, BOTH, moved(**steps))


def split(value):
    high = value.astype(BF16)
    return high, (value - high.astype(F32)).astype(BF16)


def multiply(pieces, shifts, own, partner, offset, total):
    dims = (((1,), (1,)), ((), ()))
    total[...] = jnp.zeros_like(total)

    def tile(k, carry):
        def columns(start):
            return pl.ds(pl.multiple_of(k * TILE + start, TILE), TILE)

        parts = [piece[:, columns(start)] for piece, start in zip(pieces, shifts)]
        t_high, t_low = split(jnp.concatenate(parts, axis=0))
        at = columns(offset)
        v_high, v_low = split(jnp.concatenate([own[:, at], partner[:, at]], axis=0))
        part = lax.dot_general(t_high, v_low, dims, preferred_element_type=F32)
        part += lax.dot_general(t_low, v_high, dims, preferred_element_type=F32)
        part += lax.dot_general(t_high, v_high, dims, preferred_element_type=F32)
        total[...] += part
        return carry

    lax.fori_loop(0, HALF // TILE, tile, 0)


def prepare_kernel(order, energy, pair, turn):
    row = lax.broadcasted_iota(jnp.int32, (NV, NV), 0)
    chosen = (row == order[...]).astype(BF16)
    values, dims = energy[...], (((1,), (0,)), ((), ()))
    grouped = exact(values, chosen, dims)
    lane = lax.broadcasted_iota(jnp.int32, (IRREPS, NV), 1)
    irrep = lax.broadcasted_iota(jnp.int32, (IRREPS, NV), 0)
    spread = jnp.where(lane // VH == irrep, jnp.broadcast_to(grouped, (IRREPS, NV)), 0.0)
    orbital = lax.broadcasted_iota(jnp.int32, (NV, VH * VH), 0) % VH
    spot = lax.broadcasted_iota(jnp.int32, (NV, VH * VH), 1)
    both = (spot // VH == orbital).astype(F32) + (spot % VH == orbital).astype(F32)
    pair[...] = exact(spread, both.astype(BF16), dims)
    old = lax.broadcasted_iota(jnp.int32, (VH * VH, VH * VH), 0)
    new = lax.broadcasted_iota(jnp.int32, (VH * VH, VH * VH), 1)
    turn[...] = (new == old % VH * VH + old // VH).astype(BF16)


def exact(value, whole, dims):
    high = value.astype(BF16)
    rest = value - high.astype(F32)
    middle = rest.astype(BF16)
    low = (rest - middle.astype(F32)).astype(BF16)
    result = lax.dot_general(high, whole, dims, preferred_element_type=F32)
    result += lax.dot_general(middle, whole, dims, preferred_element_type=F32)
    return result + lax.dot_general(low, whole, dims, preferred_element_type=F32)


def relayout_kernel(rows, own, up, down):
    value = rows[...].reshape(16, NP)
    own[...] = value
    up[...] = value[:8]
    down[...] = value[8:]


def touch_kernel(own, partner, mark):
    mark[...] = jnp.zeros_like(mark)


def low_pack_kernel(*refs):
    for n in range(6):
        refs[6][n * 8 : n * 8 + 8, :] = refs[n][:, :HALF]


def high_pack_kernel(below, above, far_up, far_down, up, down):
    up[:8, :] = below[:8, HALF:]
    up[8:16, :] = above[:8, HALF:]
    up[16:, :] = far_up[:, HALF:]
    down[:8, :] = below[8:, HALF:]
    down[8:16, :] = above[8:, HALF:]
    down[16:, :] = far_down[:, HALF:]


def spot():
    ia, ja = lax.axis_index("ia"), lax.axis_index("ja")
    z = ia // 4 * 4 + lax.rem(ja // 2, 4)
    return lax.rem(ia, 4), ja // 8, z, lax.rem(ja, 2)


def slot_of(dy, side, dz):
    return dy * 8 + side * 4 + dz


def first_half_kernel(slots, *refs):
    count = len(refs) - 4
    own, partner, out, total = refs[count:]
    multiply(refs[:count], [0] * count, own, partner, 0, total)
    for block, slot in enumerate(slots):
        for v in range(2):
            out[v, slot] = total[block * 8 : block * 8 + 8, v * COLS : (v + 1) * COLS]


def second_half_kernel(slots, near, *refs):
    count = len(refs) - 13
    own, partner, first = refs[count : count + 3]
    direct, crossed = refs[count + 3 : count + 7], refs[count + 7 : count + 11]
    total, sums = refs[count + 11 :]
    shifts = [HALF] * near + [0] * (count - near)
    multiply(refs[:count], shifts, own, partner, HALF, total)
    for block, slot in enumerate(slots):
        dy, at = slot // 8, slot % 8
        for v in range(2):
            value = first[v, slot] + total[block * 8 : block * 8 + 8, v * COLS : (v + 1) * COLS]
            sums[v, slot] = value
            direct[dy][at, v] = value
    x, y, z, c = spot()
    for dx in range(4):
        to = lax.rem(x + dx, 4)
        for k in range(2):
            for m in range(2):
                z_low = lax.rem(to, 2) * 2 + m
                dy = lax.rem(2 * k + to // 2 - y + 4, 4)
                up = dy * 8 + lax.rem(z - z_low + 4, 4)
                down = dy * 8 + 4 + lax.rem(z_low - z + 8, 4)
                for core in range(2):
                    v = lax.rem(c + core, 2)
                    a, b = sums[v, up], sums[v, down]
                    crossed[dx][k, m, core, 0] = jnp.concatenate([a[:4], b[:4]], axis=0)
                    crossed[dx][k, m, core, 1] = jnp.concatenate([a[4:], b[4:]], axis=0)


def z_pack_kernel(*refs):
    came, direct, outs, home, held = refs[:4], refs[4:8], refs[8:16], refs[16], refs[17]
    x, y, z, c = spot()
    for dx in range(4):
        held[dx] = came[dx][...]
    for dy in range(4):
        home[0, dy] = direct[dy][0]
        home[1, dy] = direct[dy][4]
    for d in range(8):
        to = lax.rem(z + d, 8)
        k, x_low, side = to // 4, lax.rem(to // 2, 2), lax.rem(to, 2)
        for x_high in range(2):
            dx = lax.rem(x - (2 * x_high + x_low) + 4, 4)
            for core in range(2):
                for goal in range(2):
                    parts = []
                    for m in range(2):
                        block = held[dx, k, m, core, goal]
                        parts.append(jnp.where(side == 0, block[:4], block[4:]))
                    outs[d][x_high * 2 + goal, core] = jnp.concatenate(parts, axis=0)
        if d % 4:
            for dy in range(4):
                outs[d][4 + dy] = direct[dy][4 + d if d < 4 else 8 - d]


def y_pack_kernel(*refs):
    came, outs, held = refs[:8], refs[8:12], refs[12]
    for d in range(8):
        held[d] = came[d][:4]
    x, y, z, c = spot()
    side = lax.rem(z, 2)
    for e in range(4):
        to = lax.rem(y + e, 4)
        z_high, x_high = to // 2, lax.rem(to, 2)
        for z_low in range(4):
            froms = []
            for m in range(2):
                low = lax.rem(x, 2) * 2 + m
                up = lax.rem(z_high * 4 + low + lax.rem(z_low - low + 4, 4), 8)
                down = lax.rem(z_high * 4 + low - lax.rem(low - z_low + 4, 4) + 8, 8)
                froms.append(lax.rem(z - jnp.where(side == 0, up, down) + 8, 8))
            for goal in range(2):
                for core in range(2):
                    a = held[froms[0], x_high * 2 + goal, core]
                    b = held[froms[1], x_high * 2 + goal, core]
                    outs[e][z_low, goal, core] = jnp.concatenate([a[:4], b[4:]], axis=0)


def swap_pack_kernel(*refs):
    c = spot()[3]
    for e in range(4):
        for z_low in range(4):
            refs[4][e, z_low] = refs[e][z_low, 1 - c]


def base_kernel(*refs):
    came, home, r_ref, base, held = refs[:6], refs[6], refs[7], refs[8], refs[9]
    x, y, z, c = spot()
    held[0] = home[0]
    held[4] = home[1]
    for n in range(3):
        held[5 + n] = came[n][4:]
        held[3 - n] = came[3 + n][4:]
    for dy in range(4):
        source = lax.rem(y - dy + 4, 4)
        for z_low in range(4):
            up = lax.rem(z_low - z + 8, 4)
            down = 4 + lax.rem(z - z_low + 4, 4)
            for core in range(2):
                v = lax.rem(c + core, 2)
                at = pl.ds(pl.multiple_of(source * 2048 + z_low * 512 + core * COLS, COLS), COLS)
                straight = jnp.concatenate([held[up, dy, v], held[down, dy, v]], axis=0)
                base[:, at] = r_ref[:, :, at].reshape(16, COLS) + straight


def final_kernel(*refs):
    mirror, swapped = refs[:4], refs[4]
    t_ref, base, pair, occupied, turn, residual, updated, moved_ref = refs[5:]
    x, y, z, c = spot()
    lane = lax.broadcasted_iota(jnp.int32, (16, 64), 1)
    row = lax.broadcasted_iota(jnp.int32, (16, 64), 0)
    i = (z // 4 * 4 + x) * 8 + row // 2
    j = ((y * 4 + lax.rem(z, 4)) * 2 + c) * 2 + row % 2
    first = jnp.sum(jnp.where(lane == i, occupied[...], 0.0), axis=1, keepdims=True)
    second = jnp.sum(jnp.where(lane == j, occupied[...], 0.0), axis=1, keepdims=True)
    order = (0, 2, 1, 3)
    for e in range(4):
        for z_low in range(4):
            for core in range(2):
                kept, given = mirror[e][z_low, c, core], swapped[e, z_low, core]
                a, b = jnp.where(c == 0, kept, given), jnp.where(c == 0, given, kept)
                rows = [s[m * 4 + n : m * 4 + n + 1] for m in range(2) for s in (a, b) for n in order]
                column = (z_low % 2 * 2 + core) * COLS
                group = e * 2 + z_low // 2
                moved_ref[group * 16 : group * 16 + 16, column : column + COLS] = jnp.concatenate(rows, axis=0)
    moved_ref[...] = exact(moved_ref[...], turn[...], (((1,), (0,)), ((), ())))
    for e in range(4):
        source = lax.rem(y - e + 4, 4)
        for half in range(2):
            group = e * 2 + half
            at = pl.ds(pl.multiple_of(source * 2048 + half * 1024, 1024), 1024)
            total = base[:, at] + moved_ref[group * 16 : group * 16 + 16, :]
            residual[:, :, at] = total.reshape(8, 2, 1024)
            ratio = total / (pair[pl.ds(source * 2 + half, 1), :] - first - second)
            updated[:, :, at] = t_ref[:, :, at] + ratio.reshape(8, 2, 1024)


VMEM = pl.BlockSpec(memory_space=pltpu.VMEM)


def shape(*dims):
    return jax.ShapeDtypeStruct(dims, F32)


def call(kernel, name, operands, outs, scratch=(), limit=8, cost=None):
    return pl.pallas_call(
        kernel,
        in_specs=[VMEM] * len(operands),
        out_specs=[VMEM] * len(outs),
        out_shape=[shape(*dims) if isinstance(dims, tuple) else dims for dims in outs],
        scratch_shapes=[pltpu.VMEM(dims, F32) for dims in scratch],
        compiler_params=pltpu.CompilerParams(vmem_limit_bytes=limit * 1024 * 1024),
        cost_estimate=cost,
        name=name,
    )(*operands)


def shards(amplitudes, residual_in, ladder_ints, occ_energy, virt_energy, virt_order):
    own, own_up, own_down = call(
        relayout_kernel, "relayout", [amplitudes], [(16, NP), (8, NP), (8, NP)]
    )
    pair_energy, turn = call(
        prepare_kernel,
        "prepare",
        [virt_order.reshape(1, NV), virt_energy.reshape(1, NV)],
        [(IRREPS, VH * VH), jax.ShapeDtypeStruct((VH * VH, VH * VH), BF16)],
        limit=16,
    )

    from_below, from_above = shift(own, dy=1), shift(own, dy=-1)
    up, down = [shift(own_up, dz=1)], [shift(own_down, dz=-1)]
    up.append(shift(up[-1], dz=1))
    down.append(shift(down[-1], dz=-1))
    far_up, far_down = shift(from_below[:8], dy=1), shift(from_above[8:], dy=-1)
    up[1], down[1], from_below, from_above = lax.optimization_barrier((up[1], down[1], from_below, from_above))
    up.append(shift(up[-1], dz=1))
    down.append(shift(down[-1], dz=-1))
    partner = shift(ladder_ints, dc=1)
    far_up, far_down, up[2], down[2] = lax.optimization_barrier((far_up, far_down, up[2], down[2]))

    (low,) = call(low_pack_kernel, "low_pack", up + down, [(48, HALF)])
    low_below, low_above = shift(low, dy=1), shift(low, dy=-1)
    low_far_up, low_far_down = shift(low_below[:24], dy=1), shift(low_above[24:], dy=-1)

    high_up, high_down = call(
        high_pack_kernel, "high_pack", [from_below, from_above, far_up, far_down], [(24, HALF)] * 2
    )
    high_ups, high_downs = [], []
    for hop in range(3):
        if hop == 1:
            mark = call(touch_kernel, "touch", [ladder_ints, partner], [(8, 128)])
            high_up, pair_energy, turn, mark = lax.optimization_barrier((high_up, pair_energy, turn, mark))
        high_up, high_down = shift(high_up, dz=1), shift(high_down, dz=-1)
        high_ups.append(high_up)
        high_downs.append(high_down)

    near = [own, from_below, from_above, far_up, far_down] + up + down
    near_slots = [slot_of(dy, side, 0) for dy in (0, 3, 1) for side in range(2)]
    near_slots += [slot_of(2, 0, 0), slot_of(2, 1, 0)]
    near_slots += [slot_of(0, side, dz) for side in range(2) for dz in (1, 2, 3)]
    low_pieces = [low_below, low_above, low_far_up, low_far_down]
    low_slots = [slot_of(dy, side, dz) for dy in (3, 1) for side in range(2) for dz in (1, 2, 3)]
    low_slots += [slot_of(2, side, dz) for side in range(2) for dz in (1, 2, 3)]
    high_pieces = high_ups + high_downs
    high_slots = [slot_of(dy, side, dz) for side in range(2) for dz in (1, 2, 3) for dy in (3, 1, 2)]

    cost = pl.CostEstimate(flops=2 * 3 * ROWS * 2 * COLS * HALF, bytes_accessed=12 << 20, transcendentals=0)
    sums = (2, 32, 8, COLS)
    total = (ROWS, 2 * COLS)
    (first,) = call(
        lambda *refs: first_half_kernel(near_slots + low_slots, *refs),
        "first_half",
        near + low_pieces + [ladder_ints, partner],
        [sums],
        [total],
        limit=MULTIPLY_LIMIT,
        cost=cost,
    )
    results = call(
        lambda *refs: second_half_kernel(near_slots + high_slots, len(near), *refs),
        "second_half",
        near + high_pieces + [ladder_ints, partner, first],
        [(8, 2, 8, COLS)] * 4 + [(2, 2, 2, 2, 8, COLS)] * 4,
        [total, sums],
        limit=MULTIPLY_LIMIT,
        cost=cost,
    )

    direct, crossed = results[:4], results[4:]
    came = [crossed[0]] + [shift(crossed[dx], dx=dx) for dx in range(1, 4)]
    direct = [direct[0]] + [shift(direct[dy], dy=dy) for dy in range(1, 4)]
    chunk, mixed = (4, 2, 8, COLS), (8, 2, 8, COLS)
    *z_sent, home = call(
        z_pack_kernel,
        "z_pack",
        came + direct,
        [mixed if d % 4 else chunk for d in range(8)] + [(2, 4, 2, 8, COLS)],
        [(4, 2, 2, 2, 2, 8, COLS)],
    )
    z_came = [z_sent[0]] + [shift(z_sent[d], dz=d) for d in range(1, 8)]
    y_sent = call(y_pack_kernel, "y_pack", z_came, [(4, 2, 2, 8, COLS)] * 4, [(8,) + chunk])
    mirror = [y_sent[0]] + [shift(y_sent[e], dy=e) for e in range(1, 4)]
    straight = [z_came[d] for d in (1, 2, 3, 5, 6, 7)]
    (base,) = call(base_kernel, "base", straight + [home, residual_in], [(16, NP)], [(8,) + chunk])
    (swapped,) = call(swap_pack_kernel, "swap_pack", mirror, [(4, 4, 2, 8, COLS)])
    swapped = shift(swapped, dc=1)
    residual, updated = call(
        final_kernel,
        "final",
        mirror + [swapped, amplitudes, base, pair_energy, occ_energy.reshape(1, 64), turn],
        [(8, 2, NP)] * 2,
        [(128, VH * VH)],
    )
    return residual, updated


def solution(mesh):
    placed = (P("ia", "ja", None), P("ia", "ja", None), P("ja", None), P(), P(), P())
    return jax.shard_map(
        shards,
        mesh=mesh,
        in_specs=placed,
        out_specs=(P("ia", "ja", None), P("ia", "ja", None)),
        check_vma=False,
    )
```

```python
import jax
import jax.numpy as jnp
from jax import lax
from jax.experimental import pallas as pl
from jax.experimental.pallas import tpu as pltpu
from jax.sharding import PartitionSpec as P

NV = 256
IRREPS = 8
VH = 32
NP = 8192
HALF = NP // 2
STREAMS = 2
RANGE = NP // (2 * STREAMS)
TILE = 1024
ROWS = 256
COLS = 256
BOTH = ("ia", "ja")
F32 = jnp.float32
BF16 = jnp.bfloat16
MULTIPLY_LIMIT = 12
LOADS = 4


def device_at(x, y, z, c):
    z = z % 8
    return (z // 4 * 4 + x % 4) * 32 + (y % 4) * 8 + (z % 4) * 2 + c % 2


def moved(dx=0, dy=0, dz=0, dc=0, way=0):
    pairs = []
    for x in range(4):
        for y in range(4):
            for z in range(8):
                for c in range(2):
                    sign = 1 - 2 * c * way
                    to = device_at(x + sign * dx, y + sign * dy, z + sign * dz, c + dc)
                    pairs.append((device_at(x, y, z, c), to))
    return pairs


def shift(array, **steps):
    return lax.ppermute(array, BOTH, moved(**steps))


def split(value):
    high = value.astype(BF16)
    return high, (value - high.astype(F32)).astype(BF16)


def multiply(pieces, own, partner, start, total):
    dims = (((1,), (1,)), ((), ()))

    def tile(k, carry):
        def columns(first):
            return pl.ds(pl.multiple_of(k * TILE + first, TILE), TILE)

        parts = [ref[row : row + rows, columns(first)] for ref, row, rows, first in pieces]
        t_high, t_low = split(jnp.concatenate(parts, axis=0))
        at = columns(start)
        v_high, v_low = split(jnp.concatenate([own[:, at], partner[:, at]], axis=0))
        part = lax.dot_general(t_high, v_low, dims, preferred_element_type=F32)
        part += lax.dot_general(t_low, v_high, dims, preferred_element_type=F32)
        part += lax.dot_general(t_high, v_high, dims, preferred_element_type=F32)
        total[...] += part
        return carry

    lax.fori_loop(0, RANGE // TILE, tile, 0)


def prepare_kernel(order, energy, pair, turn):
    row = lax.broadcasted_iota(jnp.int32, (NV, NV), 0)
    chosen = (row == order[...]).astype(BF16)
    values, dims = energy[...], (((1,), (0,)), ((), ()))
    grouped = exact(values, chosen, dims)
    lane = lax.broadcasted_iota(jnp.int32, (IRREPS, NV), 1)
    irrep = lax.broadcasted_iota(jnp.int32, (IRREPS, NV), 0)
    spread = jnp.where(lane // VH == irrep, jnp.broadcast_to(grouped, (IRREPS, NV)), 0.0)
    orbital = lax.broadcasted_iota(jnp.int32, (NV, VH * VH), 0) % VH
    spot = lax.broadcasted_iota(jnp.int32, (NV, VH * VH), 1)
    both = (spot // VH == orbital).astype(F32) + (spot % VH == orbital).astype(F32)
    pair[...] = exact(spread, both.astype(BF16), dims)
    old = lax.broadcasted_iota(jnp.int32, (VH * VH, VH * VH), 0)
    new = lax.broadcasted_iota(jnp.int32, (VH * VH, VH * VH), 1)
    turn[...] = (new == old % VH * VH + old // VH).astype(BF16)


def exact(value, whole, dims):
    high = value.astype(BF16)
    rest = value - high.astype(F32)
    middle = rest.astype(BF16)
    low = (rest - middle.astype(F32)).astype(BF16)
    result = lax.dot_general(high, whole, dims, preferred_element_type=F32)
    result += lax.dot_general(middle, whole, dims, preferred_element_type=F32)
    return result + lax.dot_general(low, whole, dims, preferred_element_type=F32)


def relayout_kernel(rows, own, *firsts):
    value = rows[...].reshape(16, NP)
    own[...] = value
    for stream in range(STREAMS):
        at = stream * 2 * RANGE
        low, high = value[:, at : at + RANGE], value[:, at + RANGE : at + 2 * RANGE]
        y_first, z_first = firsts[2 * stream], firsts[2 * stream + 1]
        y_first[:16, :], y_first[16:, :] = high, low
        z_first[:16, :], z_first[16:, :] = low, high


def sent_along(turn):
    near = [(1, turn - 1, 0)] if turn <= 3 else []
    return near + [(0, dy, turn - 1 - dy) for dy in range(3) if 0 <= turn - 1 - dy <= 3]


def came_along(turn):
    return [(half, dy + 1, dz) for half, dy, dz in sent_along(turn)]


def turned(blocks):
    return [(1 - half, dz, dy) for half, dy, dz in blocks]


def round_kernel(turn, y_came, z_came, y_next, z_next):
    tags = came_along(turn)
    sources = {tag: (y_came, n) for n, tag in enumerate(tags)}
    sources.update({tag: (z_came, n) for n, tag in enumerate(turned(tags))})
    wanted = sent_along(turn + 1)
    for goal, blocks in ((y_next, wanted), (z_next, turned(wanted))):
        for n, tag in enumerate(blocks):
            ref, at = sources[tag]
            goal[n * 16 : n * 16 + 16, :] = ref[at * 16 : at * 16 + 16, :]


def spot():
    ia, ja = lax.axis_index("ia"), lax.axis_index("ja")
    z = ia // 4 * 4 + lax.rem(ja // 2, 4)
    return lax.rem(ia, 4), ja // 8, z, lax.rem(ja, 2)


def stream_pieces(stream, refs):
    own, came = refs[0], refs[1:13]
    result = []
    for half in range(2):
        pieces = [(own, 0, 16, (stream * 2 + half) * RANGE)]
        slots = [0]
        for turn in range(1, 7):
            tags = came_along(turn)
            for ref, blocks in ((came[2 * turn - 2], tags), (came[2 * turn - 1], turned(tags))):
                for n, (which, dy, dz) in enumerate(blocks):
                    if which == half:
                        pieces.append((ref, n * 16, 16, 0))
                        slots.append(dy * 4 + dz)
        result.append((pieces, slots))
    return result


def product(stream, refs, own, partner, total, use):
    for half, (pieces, slots) in enumerate(stream_pieces(stream, refs)):
        total[...] = jnp.zeros_like(total)
        multiply(pieces, own, partner, (stream * 2 + half) * RANGE % HALF, total)
        for block, slot in enumerate(slots):
            for v in range(2):
                use(half, v, slot, total[block * 16 : block * 16 + 16, v * COLS : (v + 1) * COLS])


def stream_kernel(stream, *refs):
    own, partner = refs[13:15]
    out, total = refs[-2:]

    def use(half, v, slot, value):
        if half == 0:
            out[v, slot] = value if stream == 0 else refs[15][v, slot] + value
        else:
            out[v, slot] = out[v, slot] + value

    product(stream, refs, own, partner, total, use)


def load_kernel(part, source, held, ready):
    copies = []
    for n in range(LOADS):
        rows = pl.ds(n * (COLS // LOADS), COLS // LOADS)
        block = source.at[rows, part * HALF : (part + 1) * HALF]
        copies.append(pltpu.make_async_copy(block, held.at[rows], ready.at[n]))
    for copy in copies:
        copy.start()
    for copy in copies:
        copy.wait()


def last_stream_kernel(*refs):
    own, partner, first = refs[13:16]
    direct, crossed = refs[16:20], refs[20:24]
    total, sums = refs[24:]

    def use(half, v, slot, value):
        if half == 0:
            sums[v, slot] = first[v, slot] + value
        else:
            value = sums[v, slot] + value
            sums[v, slot] = value
            direct[slot // 4][slot % 4, v] = value

    product(STREAMS - 1, refs, own, partner, total, use)
    x, y, z, c = spot()
    for dx in range(4):
        to = lax.rem(x + dx, 4)
        for k in range(2):
            for m in range(2):
                z_low = lax.rem(to, 2) * 2 + m
                y_home = 2 * k + to // 2
                dy = lax.rem(jnp.where(c == 0, y - y_home, y_home - y) + 4, 4)
                dz = lax.rem(jnp.where(c == 0, z - z_low, z_low - z) + 8, 4)
                for core in range(2):
                    block = sums[lax.rem(c + core, 2), dy * 4 + dz]
                    a, b = block[:8], block[8:]
                    crossed[dx][k, m, core, 0] = jnp.concatenate([a[:4], b[:4]], axis=0)
                    crossed[dx][k, m, core, 1] = jnp.concatenate([a[4:], b[4:]], axis=0)


def z_pack_kernel(*refs):
    came, direct, outs, home, held = refs[:4], refs[4:8], refs[8:16], refs[16], refs[17]
    x, y, z, c = spot()
    for dx in range(4):
        held[dx] = came[dx][...]
    for dy in range(4):
        for half in range(2):
            for v in range(2):
                home[half, dy, v] = direct[dy][0, v, half * 8 : half * 8 + 8, :]
    for d in range(8):
        to = lax.rem(jnp.where(c == 0, z + d, z - d + 8), 8)
        k, x_low, side = to // 4, lax.rem(to // 2, 2), lax.rem(to, 2)
        for x_high in range(2):
            dx = lax.rem(x - (2 * x_high + x_low) + 4, 4)
            for core in range(2):
                for goal in range(2):
                    parts = []
                    for m in range(2):
                        block = held[dx, k, m, core, goal]
                        parts.append(jnp.where(side == 0, block[:4], block[4:]))
                    outs[d][x_high * 2 + goal, core] = jnp.concatenate(parts, axis=0)
        if d > 4:
            for half in range(2):
                for dy in range(4):
                    for v in range(2):
                        value = direct[dy][8 - d, v, half * 8 : half * 8 + 8, :]
                        outs[d][4 + half * 4 + dy, v] = value


def y_pack_kernel(*refs):
    came, outs, held = refs[:8], refs[8:12], refs[12]
    for d in range(8):
        held[d] = came[d][:4]
    x, y, z, c = spot()
    for e in range(4):
        to = lax.rem(y + e, 4)
        z_high, x_high = to // 2, lax.rem(to, 2)
        for z_low in range(4):
            froms = []
            for m in range(2):
                low = lax.rem(x, 2) * 2 + m
                up = lax.rem(z_high * 4 + low + lax.rem(z_low - low + 4, 4), 8)
                down = lax.rem(z_high * 4 + low - lax.rem(low - z_low + 4, 4) + 8, 8)
                froms.append(lax.rem(jnp.where(c == 0, z - up, down - z) + 8, 8))
            for goal in range(2):
                for core in range(2):
                    a = held[froms[0], x_high * 2 + goal, core]
                    b = held[froms[1], x_high * 2 + goal, core]
                    outs[e][z_low, goal, core] = jnp.concatenate([a[:4], b[4:]], axis=0)


def swap_pack_kernel(*refs):
    c = spot()[3]
    for e in range(4):
        for z_low in range(4):
            refs[4][e, z_low] = refs[e][z_low, 1 - c]


def base_kernel(*refs):
    came, home, r_ref, base, held = refs[:3], refs[3], refs[4], refs[5], refs[6]
    x, y, z, c = spot()
    for half in range(2):
        held[half, 0] = home[half]
        for dz in range(1, 4):
            held[half, dz] = came[3 - dz][4 + half * 4 : 8 + half * 4]
    for dy in range(4):
        source = lax.rem(jnp.where(c == 0, y + dy, y - dy + 4), 4)
        for z_low in range(4):
            dz = lax.rem(jnp.where(c == 0, z_low - z, z - z_low) + 8, 4)
            for core in range(2):
                v = lax.rem(c + core, 2)
                at = pl.ds(pl.multiple_of(source * 2048 + z_low * 512 + core * COLS, COLS), COLS)
                straight = jnp.concatenate([held[0, dz, dy, v], held[1, dz, dy, v]], axis=0)
                base[:, at] = r_ref[:, :, at].reshape(16, COLS) + straight


def final_kernel(*refs):
    mirror, swapped = refs[:4], refs[4]
    t_ref, base, pair, occupied, turn, residual, updated, moved_ref = refs[5:]
    x, y, z, c = spot()
    lane = lax.broadcasted_iota(jnp.int32, (16, 64), 1)
    row = lax.broadcasted_iota(jnp.int32, (16, 64), 0)
    i = (z // 4 * 4 + x) * 8 + row // 2
    j = ((y * 4 + lax.rem(z, 4)) * 2 + c) * 2 + row % 2
    first = jnp.sum(jnp.where(lane == i, occupied[...], 0.0), axis=1, keepdims=True)
    second = jnp.sum(jnp.where(lane == j, occupied[...], 0.0), axis=1, keepdims=True)
    order = (0, 2, 1, 3)
    for e in range(4):
        for z_low in range(4):
            for core in range(2):
                kept, given = mirror[e][z_low, c, core], swapped[e, z_low, core]
                a, b = jnp.where(c == 0, kept, given), jnp.where(c == 0, given, kept)
                rows = [s[m * 4 + n : m * 4 + n + 1] for m in range(2) for s in (a, b) for n in order]
                column = (z_low % 2 * 2 + core) * COLS
                group = e * 2 + z_low // 2
                moved_ref[group * 16 : group * 16 + 16, column : column + COLS] = jnp.concatenate(rows, axis=0)
    moved_ref[...] = exact(moved_ref[...], turn[...], (((1,), (0,)), ((), ())))
    for e in range(4):
        source = lax.rem(y - e + 4, 4)
        for half in range(2):
            group = e * 2 + half
            at = pl.ds(pl.multiple_of(source * 2048 + half * 1024, 1024), 1024)
            total = base[:, at] + moved_ref[group * 16 : group * 16 + 16, :]
            residual[:, :, at] = total.reshape(8, 2, 1024)
            ratio = total / (pair[pl.ds(source * 2 + half, 1), :] - first - second)
            updated[:, :, at] = t_ref[:, :, at] + ratio.reshape(8, 2, 1024)


VMEM = pl.BlockSpec(memory_space=pltpu.VMEM)


def shape(*dims):
    return jax.ShapeDtypeStruct(dims, F32)


def call(kernel, name, operands, outs, scratch=(), limit=8, cost=None):
    return pl.pallas_call(
        kernel,
        in_specs=[VMEM] * len(operands),
        out_specs=[VMEM] * len(outs),
        out_shape=[shape(*dims) if isinstance(dims, tuple) else dims for dims in outs],
        scratch_shapes=[pltpu.VMEM(dims, F32) for dims in scratch],
        compiler_params=pltpu.CompilerParams(vmem_limit_bytes=limit * 1024 * 1024),
        cost_estimate=cost,
        name=name,
    )(*operands)


def load(array, part):
    return pl.pallas_call(
        lambda *refs: load_kernel(part, *refs),
        in_specs=[pl.BlockSpec(memory_space=pltpu.HBM)],
        out_specs=VMEM,
        out_shape=shape(COLS, HALF),
        scratch_shapes=[pltpu.SemaphoreType.DMA((LOADS,))],
        compiler_params=pltpu.CompilerParams(vmem_limit_bytes=1024 * 1024),
        cost_estimate=pl.CostEstimate(flops=0, bytes_accessed=8 << 20, transcendentals=0),
        name="load",
    )(array)


def shards(amplitudes, residual_in, ladder_ints, occ_energy, virt_energy, virt_order):
    own, *firsts = call(
        relayout_kernel, "relayout", [amplitudes], [(16, NP)] + [(32, RANGE)] * (2 * STREAMS)
    )
    pair_energy, turn_matrix = call(
        prepare_kernel,
        "prepare",
        [virt_order.reshape(1, NV), virt_energy.reshape(1, NV)],
        [(IRREPS, VH * VH), jax.ShapeDtypeStruct((VH * VH, VH * VH), BF16)],
        limit=16,
    )

    y_next, z_next = firsts[::2], firsts[1::2]
    arrived, loaded, pending = [[] for _ in range(STREAMS)], [], None
    partner = shift(ladder_ints, dc=1)
    for turn in range(1, 7):
        for stream in range(STREAMS):
            y_came = shift(y_next[stream], dy=1, way=1)
            z_came = shift(z_next[stream], dz=1, way=1)
            arrived[stream] += [y_came, z_came]
            if turn < 6:
                rows = len(sent_along(turn + 1)) * 16
                y_next[stream], z_next[stream] = call(
                    lambda *refs, turn=turn: round_kernel(turn, *refs),
                    "round",
                    [y_came, z_came],
                    [(rows, RANGE)] * 2,
                )
            if turn == 4 and stream == 0:
                y_next[0], pair_energy, turn_matrix = lax.optimization_barrier(
                    (y_next[0], pair_energy, turn_matrix)
                )
            if turn < 6 and stream == 0 and pending is not None:
                y_next[0], pending = lax.optimization_barrier((y_next[0], pending))
                loaded.append(pending)
            if turn < 5 and stream == STREAMS - 1:
                n = turn - 1
                source = lax.optimization_barrier(((ladder_ints, partner)[n % 2], y_came))[0]
                pending = load(source, n // 2)

    cost = pl.CostEstimate(flops=2 * 3 * ROWS * 2 * COLS * 2 * RANGE, bytes_accessed=6 << 20, transcendentals=0)
    sums = (2, 16, 16, COLS)
    total = (ROWS, 2 * COLS)
    first = []
    for stream in range(STREAMS - 1):
        held = stream * 2 * RANGE // HALF * 2
        first = list(call(
            lambda *refs, stream=stream: stream_kernel(stream, *refs),
            "stream",
            [own] + arrived[stream] + loaded[held : held + 2] + first,
            [sums],
            [total],
            limit=MULTIPLY_LIMIT,
            cost=cost,
        ))
    results = call(
        last_stream_kernel,
        "last_stream",
        [own] + arrived[STREAMS - 1] + loaded[2:] + first,
        [(4, 2, 16, COLS)] * 4 + [(2, 2, 2, 2, 8, COLS)] * 4,
        [total, sums],
        limit=MULTIPLY_LIMIT,
        cost=cost,
    )

    direct, crossed = results[:4], results[4:]
    came = [crossed[0]] + [shift(crossed[dx], dx=dx) for dx in range(1, 4)]
    direct = [direct[0]] + [shift(direct[dy], dy=-dy, way=1) for dy in range(1, 4)]
    chunk, mixed = (4, 2, 8, COLS), (12, 2, 8, COLS)
    *z_sent, home = call(
        z_pack_kernel,
        "z_pack",
        came + direct,
        [mixed if d > 4 else chunk for d in range(8)] + [(2, 4, 2, 8, COLS)],
        [(4, 2, 2, 2, 2, 8, COLS)],
    )
    z_came = [z_sent[0]] + [shift(z_sent[d], dz=d, way=1) for d in range(1, 8)]
    y_sent = call(y_pack_kernel, "y_pack", z_came, [(4, 2, 2, 8, COLS)] * 4, [(8,) + chunk])
    mirror = [y_sent[0]] + [shift(y_sent[e], dy=e) for e in range(1, 4)]
    straight = z_came[5:]
    (base,) = call(base_kernel, "base", straight + [home, residual_in], [(16, NP)], [(2, 4) + chunk])
    (swapped,) = call(swap_pack_kernel, "swap_pack", mirror, [(4, 4, 2, 8, COLS)])
    swapped = shift(swapped, dc=1)
    residual, updated = call(
        final_kernel,
        "final",
        mirror + [swapped, amplitudes, base, pair_energy, occ_energy.reshape(1, 64), turn_matrix],
        [(8, 2, NP)] * 2,
        [(128, VH * VH)],
    )
    return residual, updated


def solution(mesh):
    placed = (P("ia", "ja", None), P("ia", "ja", None), P("ja", None), P(), P(), P())
    return jax.shard_map(
        shards,
        mesh=mesh,
        in_specs=placed,
        out_specs=(P("ia", "ja", None), P("ia", "ja", None)),
        check_vma=False,
    )
```

```python
import jax
import jax.numpy as jnp
from jax import lax
from jax.experimental import pallas as pl
from jax.experimental.pallas import tpu as pltpu
from jax.sharding import PartitionSpec as P

NV = 256
IRREPS = 8
VH = 32
NP = 8192
HALF = NP // 2
STREAMS = 2
RANGE = NP // (2 * STREAMS)
TILE = 512
ROWS = 256
COLS = 256
BOTH = ("ia", "ja")
F32 = jnp.float32
BF16 = jnp.bfloat16
MULTIPLY_LIMIT = 12
LOADS = 4


def device_at(x, y, z, c):
    z = z % 8
    return (z // 4 * 4 + x % 4) * 32 + (y % 4) * 8 + (z % 4) * 2 + c % 2


def moved(dx=0, dy=0, dz=0, dc=0, way=0):
    pairs = []
    for x in range(4):
        for y in range(4):
            for z in range(8):
                for c in range(2):
                    sign = 1 - 2 * c * way
                    to = device_at(x + sign * dx, y + sign * dy, z + sign * dz, c + dc)
                    pairs.append((device_at(x, y, z, c), to))
    return pairs


def shift(array, **steps):
    return lax.ppermute(array, BOTH, moved(**steps))


def split(value):
    high = value.astype(BF16)
    return high, (value - high.astype(F32)).astype(BF16)


def multiply(pieces, own, partner, start, total):
    dims = (((1,), (1,)), ((), ()))

    def tile(k, carry):
        def columns(first):
            return pl.ds(pl.multiple_of(k * TILE + first, TILE), TILE)

        parts = [ref[row : row + rows, columns(first)] for ref, row, rows, first in pieces]
        t_high, t_low = split(jnp.concatenate(parts, axis=0))
        at = columns(start)
        v_high, v_low = split(jnp.concatenate([own[:, at], partner[:, at]], axis=0))
        part = lax.dot_general(t_high, v_low, dims, preferred_element_type=F32)
        part += lax.dot_general(t_low, v_high, dims, preferred_element_type=F32)
        part += lax.dot_general(t_high, v_high, dims, preferred_element_type=F32)
        total[...] += part
        return carry

    lax.fori_loop(0, RANGE // TILE, tile, 0)


def prepare_kernel(order, energy, pair, turn):
    row = lax.broadcasted_iota(jnp.int32, (NV, NV), 0)
    chosen = (row == order[...]).astype(BF16)
    values, dims = energy[...], (((1,), (0,)), ((), ()))
    grouped = exact(values, chosen, dims)
    lane = lax.broadcasted_iota(jnp.int32, (IRREPS, NV), 1)
    irrep = lax.broadcasted_iota(jnp.int32, (IRREPS, NV), 0)
    spread = jnp.where(lane // VH == irrep, jnp.broadcast_to(grouped, (IRREPS, NV)), 0.0)
    orbital = lax.broadcasted_iota(jnp.int32, (NV, VH * VH), 0) % VH
    spot = lax.broadcasted_iota(jnp.int32, (NV, VH * VH), 1)
    both = (spot // VH == orbital).astype(F32) + (spot % VH == orbital).astype(F32)
    pair[...] = exact(spread, both.astype(BF16), dims)
    new = lax.broadcasted_iota(jnp.int32, (128, VH * VH), 1)

    def rows(n, carry):
        old = lax.broadcasted_iota(jnp.int32, (128, VH * VH), 0) + n * 128
        turn[pl.ds(pl.multiple_of(n * 128, 128), 128), :] = (new == old % VH * VH + old // VH).astype(BF16)
        return carry

    lax.fori_loop(0, VH * VH // 128, rows, 0)


def exact(value, whole, dims):
    high = value.astype(BF16)
    rest = value - high.astype(F32)
    middle = rest.astype(BF16)
    low = (rest - middle.astype(F32)).astype(BF16)
    result = lax.dot_general(high, whole, dims, preferred_element_type=F32)
    result += lax.dot_general(middle, whole, dims, preferred_element_type=F32)
    return result + lax.dot_general(low, whole, dims, preferred_element_type=F32)


def relayout_kernel(rows, own, *firsts):
    def columns(k, carry):
        at = pl.ds(pl.multiple_of(k * 256, 256), 256)
        for part in range(2 * STREAMS):
            from_at = pl.ds(pl.multiple_of(k * 256 + part * RANGE, 256), 256)
            value = rows[:, :, from_at].reshape(16, 256)
            own[:, from_at] = value
            half = part % 2
            y_first, z_first = firsts[part // 2 * 2], firsts[part // 2 * 2 + 1]
            y_first[16 - 16 * half : 32 - 16 * half, at] = value
            z_first[16 * half : 16 * half + 16, at] = value
        return carry

    lax.fori_loop(0, RANGE // 256, columns, 0)


def sent_along(turn):
    near = [(1, turn - 1, 0)] if turn <= 3 else []
    return near + [(0, dy, turn - 1 - dy) for dy in range(3) if 0 <= turn - 1 - dy <= 3]


def came_along(turn):
    return [(half, dy + 1, dz) for half, dy, dz in sent_along(turn)]


def turned(blocks):
    return [(1 - half, dz, dy) for half, dy, dz in blocks]


def round_kernel(turn, y_came, z_came, y_next, z_next):
    tags = came_along(turn)
    sources = {tag: (y_came, n) for n, tag in enumerate(tags)}
    sources.update({tag: (z_came, n) for n, tag in enumerate(turned(tags))})
    wanted = sent_along(turn + 1)

    def columns(k, carry):
        at_columns = pl.ds(pl.multiple_of(k * 256, 256), 256)
        for goal, blocks in ((y_next, wanted), (z_next, turned(wanted))):
            for n, tag in enumerate(blocks):
                ref, at = sources[tag]
                goal[n * 16 : n * 16 + 16, at_columns] = ref[at * 16 : at * 16 + 16, at_columns]
        return carry

    lax.fori_loop(0, RANGE // 256, columns, 0)


def spot():
    ia, ja = lax.axis_index("ia"), lax.axis_index("ja")
    z = ia // 4 * 4 + lax.rem(ja // 2, 4)
    return lax.rem(ia, 4), ja // 8, z, lax.rem(ja, 2)


def stream_pieces(stream, refs):
    own, came = refs[0], refs[1:13]
    result = []
    for half in range(2):
        pieces = [(own, 0, 16, (stream * 2 + half) * RANGE)]
        slots = [0]
        for turn in range(1, 7):
            tags = came_along(turn)
            for ref, blocks in ((came[2 * turn - 2], tags), (came[2 * turn - 1], turned(tags))):
                for n, (which, dy, dz) in enumerate(blocks):
                    if which == half:
                        pieces.append((ref, n * 16, 16, 0))
                        slots.append(dy * 4 + dz)
        result.append((pieces, slots))
    return result


def product(stream, refs, own, partner, total, use):
    for half, (pieces, slots) in enumerate(stream_pieces(stream, refs)):
        total[...] = jnp.zeros_like(total)
        multiply(pieces, own, partner, (stream * 2 + half) * RANGE % HALF, total)
        for block, slot in enumerate(slots):
            for v in range(2):
                use(half, v, slot, total[block * 16 : block * 16 + 16, v * COLS : (v + 1) * COLS])


def stream_kernel(stream, *refs):
    own, partner = refs[13:15]
    out, total = refs[-2:]

    def use(half, v, slot, value):
        if half == 0:
            out[v, slot] = value if stream == 0 else refs[15][v, slot] + value
        else:
            out[v, slot] = out[v, slot] + value

    product(stream, refs, own, partner, total, use)


def load_kernel(part, source, held, ready):
    copies = []
    for n in range(LOADS):
        rows = pl.ds(n * (COLS // LOADS), COLS // LOADS)
        block = source.at[rows, part * HALF : (part + 1) * HALF]
        copies.append(pltpu.make_async_copy(block, held.at[rows], ready.at[n]))
    for copy in copies:
        copy.start()
    for copy in copies:
        copy.wait()


def last_stream_kernel(*refs):
    own, partner, first = refs[13:16]
    direct, crossed = refs[16:20], refs[20:24]
    total, sums = refs[24:]

    def use(half, v, slot, value):
        if half == 0:
            sums[v, slot] = first[v, slot] + value
        else:
            value = sums[v, slot] + value
            sums[v, slot] = value
            direct[slot // 4][slot % 4, v] = value

    product(STREAMS - 1, refs, own, partner, total, use)
    x, y, z, c = spot()
    for dx in range(4):
        to = lax.rem(x + dx, 4)
        for k in range(2):
            for m in range(2):
                z_low = lax.rem(to, 2) * 2 + m
                y_home = 2 * k + to // 2
                dy = lax.rem(jnp.where(c == 0, y - y_home, y_home - y) + 4, 4)
                dz = lax.rem(jnp.where(c == 0, z - z_low, z_low - z) + 8, 4)
                for core in range(2):
                    block = sums[lax.rem(c + core, 2), dy * 4 + dz]
                    a, b = block[:8], block[8:]
                    crossed[dx][k, m, core, 0] = jnp.concatenate([a[:4], b[:4]], axis=0)
                    crossed[dx][k, m, core, 1] = jnp.concatenate([a[4:], b[4:]], axis=0)


def z_pack_kernel(*refs):
    came, direct, outs, home, held = refs[:4], refs[4:8], refs[8:16], refs[16], refs[17]
    x, y, z, c = spot()
    for dx in range(4):
        held[dx] = came[dx][...]
    for dy in range(4):
        for half in range(2):
            for v in range(2):
                home[half, dy, v] = direct[dy][0, v, half * 8 : half * 8 + 8, :]
    for d in range(8):
        to = lax.rem(jnp.where(c == 0, z + d, z - d + 8), 8)
        k, x_low, side = to // 4, lax.rem(to // 2, 2), lax.rem(to, 2)
        for x_high in range(2):
            dx = lax.rem(x - (2 * x_high + x_low) + 4, 4)
            for core in range(2):
                for goal in range(2):
                    parts = []
                    for m in range(2):
                        block = held[dx, k, m, core, goal]
                        parts.append(jnp.where(side == 0, block[:4], block[4:]))
                    outs[d][x_high * 2 + goal, core] = jnp.concatenate(parts, axis=0)
        if d > 4:
            for half in range(2):
                for dy in range(4):
                    for v in range(2):
                        value = direct[dy][8 - d, v, half * 8 : half * 8 + 8, :]
                        outs[d][4 + half * 4 + dy, v] = value


def y_pack_kernel(*refs):
    came, outs, held = refs[:8], refs[8:12], refs[12]
    for d in range(8):
        held[d] = came[d][:4]
    x, y, z, c = spot()
    for e in range(4):
        to = lax.rem(y + e, 4)
        z_high, x_high = to // 2, lax.rem(to, 2)
        for z_low in range(4):
            froms = []
            for m in range(2):
                low = lax.rem(x, 2) * 2 + m
                up = lax.rem(z_high * 4 + low + lax.rem(z_low - low + 4, 4), 8)
                down = lax.rem(z_high * 4 + low - lax.rem(low - z_low + 4, 4) + 8, 8)
                froms.append(lax.rem(jnp.where(c == 0, z - up, down - z) + 8, 8))
            for goal in range(2):
                for core in range(2):
                    a = held[froms[0], x_high * 2 + goal, core]
                    b = held[froms[1], x_high * 2 + goal, core]
                    outs[e][z_low, goal, core] = jnp.concatenate([a[:4], b[4:]], axis=0)


def swap_pack_kernel(*refs):
    c = spot()[3]
    for e in range(4):
        for z_low in range(4):
            refs[4][e, z_low] = refs[e][z_low, 1 - c]


def base_kernel(*refs):
    came, home, r_ref, base, held = refs[:3], refs[3], refs[4], refs[5], refs[6]
    x, y, z, c = spot()
    for half in range(2):
        held[half, 0] = home[half]
        for dz in range(1, 4):
            held[half, dz] = came[3 - dz][4 + half * 4 : 8 + half * 4]
    for dy in range(4):
        source = lax.rem(jnp.where(c == 0, y + dy, y - dy + 4), 4)
        for z_low in range(4):
            dz = lax.rem(jnp.where(c == 0, z_low - z, z - z_low) + 8, 4)
            for core in range(2):
                v = lax.rem(c + core, 2)
                at = pl.ds(pl.multiple_of(source * 2048 + z_low * 512 + core * COLS, COLS), COLS)
                straight = jnp.concatenate([held[0, dz, dy, v], held[1, dz, dy, v]], axis=0)
                base[:, at] = r_ref[:, :, at].reshape(16, COLS) + straight


def final_kernel(*refs):
    mirror, swapped = refs[:4], refs[4]
    t_ref, base, pair, occupied, turn, residual, updated, moved_ref, turned_ref = refs[5:]
    x, y, z, c = spot()
    lane = lax.broadcasted_iota(jnp.int32, (16, 64), 1)
    row = lax.broadcasted_iota(jnp.int32, (16, 64), 0)
    i = (z // 4 * 4 + x) * 8 + row // 2
    j = ((y * 4 + lax.rem(z, 4)) * 2 + c) * 2 + row % 2
    first = jnp.sum(jnp.where(lane == i, occupied[...], 0.0), axis=1, keepdims=True)
    second = jnp.sum(jnp.where(lane == j, occupied[...], 0.0), axis=1, keepdims=True)
    order = (0, 2, 1, 3)
    for e in range(4):
        for z_low in range(4):
            for core in range(2):
                kept, given = mirror[e][z_low, c, core], swapped[e, z_low, core]
                a, b = jnp.where(c == 0, kept, given), jnp.where(c == 0, given, kept)
                rows = [s[m * 4 + n : m * 4 + n + 1] for m in range(2) for s in (a, b) for n in order]
                column = (z_low % 2 * 2 + core) * COLS
                group = e * 2 + z_low // 2
                moved_ref[group * 16 : group * 16 + 16, column : column + COLS] = jnp.concatenate(rows, axis=0)
    value = moved_ref[...]

    def columns(n, carry):
        at = pl.ds(pl.multiple_of(n * 256, 256), 256)
        turned_ref[:, at] = exact(value, turn[:, at], (((1,), (0,)), ((), ())))
        return carry

    lax.fori_loop(0, VH * VH // 256, columns, 0)
    for e in range(4):
        source = lax.rem(y - e + 4, 4)
        for half in range(2):
            group = e * 2 + half
            at = pl.ds(pl.multiple_of(source * 2048 + half * 1024, 1024), 1024)
            total = base[:, at] + turned_ref[group * 16 : group * 16 + 16, :]
            residual[:, :, at] = total.reshape(8, 2, 1024)
            ratio = total / (pair[pl.ds(source * 2 + half, 1), :] - first - second)
            updated[:, :, at] = t_ref[:, :, at] + ratio.reshape(8, 2, 1024)


VMEM = pl.BlockSpec(memory_space=pltpu.VMEM)


def shape(*dims):
    return jax.ShapeDtypeStruct(dims, F32)


def call(kernel, name, operands, outs, scratch=(), limit=8, cost=None):
    return pl.pallas_call(
        kernel,
        in_specs=[VMEM] * len(operands),
        out_specs=[VMEM] * len(outs),
        out_shape=[shape(*dims) if isinstance(dims, tuple) else dims for dims in outs],
        scratch_shapes=[pltpu.VMEM(dims, F32) for dims in scratch],
        compiler_params=pltpu.CompilerParams(vmem_limit_bytes=limit * 1024 * 1024),
        cost_estimate=cost,
        name=name,
    )(*operands)


def load(array, part):
    return pl.pallas_call(
        lambda *refs: load_kernel(part, *refs),
        in_specs=[pl.BlockSpec(memory_space=pltpu.HBM)],
        out_specs=VMEM,
        out_shape=shape(COLS, HALF),
        scratch_shapes=[pltpu.SemaphoreType.DMA((LOADS,))],
        compiler_params=pltpu.CompilerParams(vmem_limit_bytes=1024 * 1024),
        cost_estimate=pl.CostEstimate(flops=0, bytes_accessed=8 << 20, transcendentals=0),
        name="load",
    )(array)


def shards(amplitudes, residual_in, ladder_ints, occ_energy, virt_energy, virt_order):
    own, *firsts = call(
        relayout_kernel, "relayout", [amplitudes], [(16, NP)] + [(32, RANGE)] * (2 * STREAMS)
    )
    pair_energy, turn_matrix = call(
        prepare_kernel,
        "prepare",
        [virt_order.reshape(1, NV), virt_energy.reshape(1, NV)],
        [(IRREPS, VH * VH), jax.ShapeDtypeStruct((VH * VH, VH * VH), BF16)],
        limit=16,
    )

    y_next, z_next = firsts[::2], firsts[1::2]
    arrived, loaded, pending = [[] for _ in range(STREAMS)], [], None
    partner = shift(ladder_ints, dc=1)
    for turn in range(1, 7):
        for stream in range(STREAMS):
            y_came = shift(y_next[stream], dy=1, way=1)
            z_came = shift(z_next[stream], dz=1, way=1)
            arrived[stream] += [y_came, z_came]
            if turn < 6:
                rows = len(sent_along(turn + 1)) * 16
                y_next[stream], z_next[stream] = call(
                    lambda *refs, turn=turn: round_kernel(turn, *refs),
                    "round",
                    [y_came, z_came],
                    [(rows, RANGE)] * 2,
                )
            if turn == 4 and stream == 0:
                y_next[0], pair_energy, turn_matrix = lax.optimization_barrier(
                    (y_next[0], pair_energy, turn_matrix)
                )
            if turn < 6 and stream == 0 and pending is not None:
                y_next[0], pending = lax.optimization_barrier((y_next[0], pending))
                loaded.append(pending)
            if turn < 5 and stream == STREAMS - 1:
                n = turn - 1
                source = lax.optimization_barrier(((ladder_ints, partner)[n % 2], y_came))[0]
                pending = load(source, n // 2)

    cost = pl.CostEstimate(flops=2 * 3 * ROWS * 2 * COLS * 2 * RANGE, bytes_accessed=6 << 20, transcendentals=0)
    sums = (2, 16, 16, COLS)
    total = (ROWS, 2 * COLS)
    first = []
    for stream in range(STREAMS - 1):
        held = stream * 2 * RANGE // HALF * 2
        first = list(call(
            lambda *refs, stream=stream: stream_kernel(stream, *refs),
            "stream",
            [own] + arrived[stream] + loaded[held : held + 2] + first,
            [sums],
            [total],
            limit=MULTIPLY_LIMIT,
            cost=cost,
        ))
    results = call(
        last_stream_kernel,
        "last_stream",
        [own] + arrived[STREAMS - 1] + loaded[2:] + first,
        [(4, 2, 16, COLS)] * 4 + [(2, 2, 2, 2, 8, COLS)] * 4,
        [total, sums],
        limit=MULTIPLY_LIMIT,
        cost=cost,
    )

    direct, crossed = results[:4], results[4:]
    came = [crossed[0]] + [shift(crossed[dx], dx=dx) for dx in range(1, 4)]
    direct = [direct[0]] + [shift(direct[dy], dy=-dy, way=1) for dy in range(1, 4)]
    chunk, mixed = (4, 2, 8, COLS), (12, 2, 8, COLS)
    *z_sent, home = call(
        z_pack_kernel,
        "z_pack",
        came + direct,
        [mixed if d > 4 else chunk for d in range(8)] + [(2, 4, 2, 8, COLS)],
        [(4, 2, 2, 2, 2, 8, COLS)],
    )
    z_came = [z_sent[0]] + [shift(z_sent[d], dz=d, way=1) for d in range(1, 8)]
    y_sent = call(y_pack_kernel, "y_pack", z_came, [(4, 2, 2, 8, COLS)] * 4, [(8,) + chunk])
    mirror = [y_sent[0]] + [shift(y_sent[e], dy=e) for e in range(1, 4)]
    straight = z_came[5:]
    (base,) = call(base_kernel, "base", straight + [home, residual_in], [(16, NP)], [(2, 4) + chunk])
    (swapped,) = call(swap_pack_kernel, "swap_pack", mirror, [(4, 4, 2, 8, COLS)])
    swapped = shift(swapped, dc=1)
    residual, updated = call(
        final_kernel,
        "final",
        mirror + [swapped, amplitudes, base, pair_energy, occ_energy.reshape(1, 64), turn_matrix],
        [(8, 2, NP)] * 2,
        [(128, VH * VH)] * 2,
    )
    return residual, updated


def solution(mesh):
    placed = (P("ia", "ja", None), P("ia", "ja", None), P("ja", None), P(), P(), P())
    return jax.shard_map(
        shards,
        mesh=mesh,
        in_specs=placed,
        out_specs=(P("ia", "ja", None), P("ia", "ja", None)),
        check_vma=False,
    )
```

```python
import jax
import jax.numpy as jnp
from jax import lax
from jax.experimental import pallas as pl
from jax.experimental.pallas import tpu as pltpu
from jax.sharding import PartitionSpec as P

NV = 256
IRREPS = 8
VH = 32
NP = 8192
HALF = NP // 2
STREAMS = 2
RANGE = NP // (2 * STREAMS)
TILE = 1024
ROWS = 256
COLS = 256
BOTH = ("ia", "ja")
F32 = jnp.float32
BF16 = jnp.bfloat16
MULTIPLY_LIMIT = 12
LOADS = 4


def device_at(x, y, z, c):
    z = z % 8
    return (z // 4 * 4 + x % 4) * 32 + (y % 4) * 8 + (z % 4) * 2 + c % 2


def moved(dx=0, dy=0, dz=0, dc=0, way=0):
    pairs = []
    for x in range(4):
        for y in range(4):
            for z in range(8):
                for c in range(2):
                    sign = 1 - 2 * c * way
                    to = device_at(x + sign * dx, y + sign * dy, z + sign * dz, c + dc)
                    pairs.append((device_at(x, y, z, c), to))
    return pairs


def shift(array, **steps):
    return lax.ppermute(array, BOTH, moved(**steps))


def split(value):
    high = value.astype(BF16)
    return high, (value - high.astype(F32)).astype(BF16)


def multiply(pieces, own, partner, start, total, width):
    dims = (((1,), (1,)), ((), ()))

    def tile(k, carry):
        def columns(first):
            return pl.ds(pl.multiple_of(k * width + first, width), width)

        parts = [ref[row : row + rows, columns(first)] for ref, row, rows, first in pieces]
        t_high, t_low = split(jnp.concatenate(parts, axis=0))
        at = columns(start)
        v_high, v_low = split(jnp.concatenate([own[:, at], partner[:, at]], axis=0))
        part = lax.dot_general(t_high, v_low, dims, preferred_element_type=F32)
        part += lax.dot_general(t_low, v_high, dims, preferred_element_type=F32)
        part += lax.dot_general(t_high, v_high, dims, preferred_element_type=F32)
        total[...] += part
        return carry

    lax.fori_loop(0, RANGE // width, tile, 0)


def prepare_kernel(order, energy, pair, turn):
    row = lax.broadcasted_iota(jnp.int32, (NV, NV), 0)
    chosen = (row == order[...]).astype(BF16)
    values, dims = energy[...], (((1,), (0,)), ((), ()))
    grouped = exact(values, chosen, dims)
    lane = lax.broadcasted_iota(jnp.int32, (IRREPS, NV), 1)
    irrep = lax.broadcasted_iota(jnp.int32, (IRREPS, NV), 0)
    spread = jnp.where(lane // VH == irrep, jnp.broadcast_to(grouped, (IRREPS, NV)), 0.0)
    orbital = lax.broadcasted_iota(jnp.int32, (NV, VH * VH), 0) % VH
    spot = lax.broadcasted_iota(jnp.int32, (NV, VH * VH), 1)
    both = (spot // VH == orbital).astype(F32) + (spot % VH == orbital).astype(F32)
    pair[...] = exact(spread, both.astype(BF16), dims)
    new = lax.broadcasted_iota(jnp.int32, (128, VH * VH), 1)

    def rows(n, carry):
        old = lax.broadcasted_iota(jnp.int32, (128, VH * VH), 0) + n * 128
        turn[pl.ds(pl.multiple_of(n * 128, 128), 128), :] = (new == old % VH * VH + old // VH).astype(BF16)
        return carry

    lax.fori_loop(0, VH * VH // 128, rows, 0)


def exact(value, whole, dims):
    high = value.astype(BF16)
    rest = value - high.astype(F32)
    middle = rest.astype(BF16)
    low = (rest - middle.astype(F32)).astype(BF16)
    result = lax.dot_general(high, whole, dims, preferred_element_type=F32)
    result += lax.dot_general(middle, whole, dims, preferred_element_type=F32)
    return result + lax.dot_general(low, whole, dims, preferred_element_type=F32)


def relayout_kernel(rows, own, *firsts):
    def columns(k, carry):
        at = pl.ds(pl.multiple_of(k * 256, 256), 256)
        for part in range(2 * STREAMS):
            from_at = pl.ds(pl.multiple_of(k * 256 + part * RANGE, 256), 256)
            value = rows[:, :, from_at].reshape(16, 256)
            own[:, from_at] = value
            half = part % 2
            y_first, z_first = firsts[part // 2 * 2], firsts[part // 2 * 2 + 1]
            y_first[16 - 16 * half : 32 - 16 * half, at] = value
            z_first[16 * half : 16 * half + 16, at] = value
        return carry

    lax.fori_loop(0, RANGE // 256, columns, 0)


def sent_along(turn):
    near = [(1, turn - 1, 0)] if turn <= 3 else []
    return near + [(0, dy, turn - 1 - dy) for dy in range(3) if 0 <= turn - 1 - dy <= 3]


def came_along(turn):
    return [(half, dy + 1, dz) for half, dy, dz in sent_along(turn)]


def turned(blocks):
    return [(1 - half, dz, dy) for half, dy, dz in blocks]


def round_kernel(turn, y_came, z_came, y_next, z_next):
    tags = came_along(turn)
    sources = {tag: (y_came, n) for n, tag in enumerate(tags)}
    sources.update({tag: (z_came, n) for n, tag in enumerate(turned(tags))})
    wanted = sent_along(turn + 1)

    def columns(k, carry):
        at_columns = pl.ds(pl.multiple_of(k * 256, 256), 256)
        for goal, blocks in ((y_next, wanted), (z_next, turned(wanted))):
            for n, tag in enumerate(blocks):
                ref, at = sources[tag]
                goal[n * 16 : n * 16 + 16, at_columns] = ref[at * 16 : at * 16 + 16, at_columns]
        return carry

    lax.fori_loop(0, RANGE // 256, columns, 0)


def spot():
    ia, ja = lax.axis_index("ia"), lax.axis_index("ja")
    z = ia // 4 * 4 + lax.rem(ja // 2, 4)
    return lax.rem(ia, 4), ja // 8, z, lax.rem(ja, 2)


def stream_pieces(stream, refs):
    own, came = refs[0], refs[1:13]
    result = []
    for half in range(2):
        pieces = [(own, 0, 16, (stream * 2 + half) * RANGE)]
        slots = [0]
        for turn in range(1, 7):
            tags = came_along(turn)
            for ref, blocks in ((came[2 * turn - 2], tags), (came[2 * turn - 1], turned(tags))):
                for n, (which, dy, dz) in enumerate(blocks):
                    if which == half:
                        pieces.append((ref, n * 16, 16, 0))
                        slots.append(dy * 4 + dz)
        result.append((pieces, slots))
    return result


def product(stream, refs, own, partner, total, use):
    for half, (pieces, slots) in enumerate(stream_pieces(stream, refs)):
        total[...] = jnp.zeros_like(total)
        width = TILE if stream == STREAMS - 1 else TILE // 2
        multiply(pieces, own, partner, (stream * 2 + half) * RANGE % HALF, total, width)
        for block, slot in enumerate(slots):
            for v in range(2):
                use(half, v, slot, total[block * 16 : block * 16 + 16, v * COLS : (v + 1) * COLS])


def stream_kernel(stream, *refs):
    own, partner = refs[13:15]
    out, total = refs[-2:]

    def use(half, v, slot, value):
        if half == 0:
            out[v, slot] = value if stream == 0 else refs[15][v, slot] + value
        else:
            out[v, slot] = out[v, slot] + value

    product(stream, refs, own, partner, total, use)


def load_kernel(part, source, held, ready):
    copies = []
    for n in range(LOADS):
        rows = pl.ds(n * (COLS // LOADS), COLS // LOADS)
        block = source.at[rows, part * HALF : (part + 1) * HALF]
        copies.append(pltpu.make_async_copy(block, held.at[rows], ready.at[n]))
    for copy in copies:
        copy.start()
    for copy in copies:
        copy.wait()


def last_stream_kernel(*refs):
    own, partner, first = refs[13:16]
    direct, crossed = refs[16:20], refs[20:24]
    total, sums = refs[24:]

    def use(half, v, slot, value):
        if half == 0:
            sums[v, slot] = first[v, slot] + value
        else:
            value = sums[v, slot] + value
            sums[v, slot] = value
            direct[slot // 4][slot % 4, v] = value

    product(STREAMS - 1, refs, own, partner, total, use)
    x, y, z, c = spot()
    for dx in range(4):
        to = lax.rem(x + dx, 4)
        for k in range(2):
            for m in range(2):
                z_low = lax.rem(to, 2) * 2 + m
                y_home = 2 * k + to // 2
                dy = lax.rem(jnp.where(c == 0, y - y_home, y_home - y) + 4, 4)
                dz = lax.rem(jnp.where(c == 0, z - z_low, z_low - z) + 8, 4)
                for core in range(2):
                    block = sums[lax.rem(c + core, 2), dy * 4 + dz]
                    a, b = block[:8], block[8:]
                    crossed[dx][k, m, core, 0] = jnp.concatenate([a[:4], b[:4]], axis=0)
                    crossed[dx][k, m, core, 1] = jnp.concatenate([a[4:], b[4:]], axis=0)


def z_pack_kernel(*refs):
    came, direct, outs, home, held = refs[:4], refs[4:8], refs[8:16], refs[16], refs[17]
    x, y, z, c = spot()
    for dx in range(4):
        held[dx] = came[dx][...]
    for dy in range(4):
        for half in range(2):
            for v in range(2):
                home[half, dy, v] = direct[dy][0, v, half * 8 : half * 8 + 8, :]
    for d in range(8):
        to = lax.rem(jnp.where(c == 0, z + d, z - d + 8), 8)
        k, x_low, side = to // 4, lax.rem(to // 2, 2), lax.rem(to, 2)
        for x_high in range(2):
            dx = lax.rem(x - (2 * x_high + x_low) + 4, 4)
            for core in range(2):
                for goal in range(2):
                    parts = []
                    for m in range(2):
                        block = held[dx, k, m, core, goal]
                        parts.append(jnp.where(side == 0, block[:4], block[4:]))
                    outs[d][x_high * 2 + goal, core] = jnp.concatenate(parts, axis=0)
        if d > 4:
            for half in range(2):
                for dy in range(4):
                    for v in range(2):
                        value = direct[dy][8 - d, v, half * 8 : half * 8 + 8, :]
                        outs[d][4 + half * 4 + dy, v] = value


def y_pack_kernel(*refs):
    came, outs, held = refs[:8], refs[8:12], refs[12]
    for d in range(8):
        held[d] = came[d][:4]
    x, y, z, c = spot()
    for e in range(4):
        to = lax.rem(y + e, 4)
        z_high, x_high = to // 2, lax.rem(to, 2)
        for z_low in range(4):
            froms = []
            for m in range(2):
                low = lax.rem(x, 2) * 2 + m
                up = lax.rem(z_high * 4 + low + lax.rem(z_low - low + 4, 4), 8)
                down = lax.rem(z_high * 4 + low - lax.rem(low - z_low + 4, 4) + 8, 8)
                froms.append(lax.rem(jnp.where(c == 0, z - up, down - z) + 8, 8))
            for goal in range(2):
                for core in range(2):
                    a = held[froms[0], x_high * 2 + goal, core]
                    b = held[froms[1], x_high * 2 + goal, core]
                    outs[e][z_low, goal, core] = jnp.concatenate([a[:4], b[4:]], axis=0)


def swap_pack_kernel(*refs):
    c = spot()[3]
    for e in range(4):
        for z_low in range(4):
            refs[4][e, z_low] = refs[e][z_low, 1 - c]


def base_kernel(*refs):
    came, home, r_ref, base, held = refs[:3], refs[3], refs[4], refs[5], refs[6]
    x, y, z, c = spot()
    for half in range(2):
        held[half, 0] = home[half]
        for dz in range(1, 4):
            held[half, dz] = came[3 - dz][4 + half * 4 : 8 + half * 4]
    for dy in range(4):
        source = lax.rem(jnp.where(c == 0, y + dy, y - dy + 4), 4)
        for z_low in range(4):
            dz = lax.rem(jnp.where(c == 0, z_low - z, z - z_low) + 8, 4)
            for core in range(2):
                v = lax.rem(c + core, 2)
                at = pl.ds(pl.multiple_of(source * 2048 + z_low * 512 + core * COLS, COLS), COLS)
                straight = jnp.concatenate([held[0, dz, dy, v], held[1, dz, dy, v]], axis=0)
                base[:, at] = r_ref[:, :, at].reshape(16, COLS) + straight


def final_kernel(*refs):
    mirror, swapped = refs[:4], refs[4]
    t_ref, base, pair, occupied, turn, residual, updated, moved_ref, turned_ref = refs[5:]
    x, y, z, c = spot()
    lane = lax.broadcasted_iota(jnp.int32, (16, 64), 1)
    row = lax.broadcasted_iota(jnp.int32, (16, 64), 0)
    i = (z // 4 * 4 + x) * 8 + row // 2
    j = ((y * 4 + lax.rem(z, 4)) * 2 + c) * 2 + row % 2
    first = jnp.sum(jnp.where(lane == i, occupied[...], 0.0), axis=1, keepdims=True)
    second = jnp.sum(jnp.where(lane == j, occupied[...], 0.0), axis=1, keepdims=True)
    order = (0, 2, 1, 3)

    def gather(n, carry):
        z_low, core = n // 2, lax.rem(n, 2)
        column = pl.ds(pl.multiple_of((lax.rem(z_low, 2) * 2 + core) * COLS, COLS), COLS)
        for e in range(4):
            kept, given = mirror[e][z_low, c, core], swapped[e, z_low, core]
            a, b = jnp.where(c == 0, kept, given), jnp.where(c == 0, given, kept)
            rows = [half[m * 4 + r : m * 4 + r + 1] for m in range(2) for half in (a, b) for r in order]
            at_rows = pl.ds(pl.multiple_of((e * 2 + z_low // 2) * 16, 16), 16)
            moved_ref[at_rows, column] = jnp.concatenate(rows, axis=0)
        return carry

    lax.fori_loop(0, 8, gather, 0)
    value = moved_ref[...]

    def columns(n, carry):
        at = pl.ds(pl.multiple_of(n * 256, 256), 256)
        turned_ref[:, at] = exact(value, turn[:, at], (((1,), (0,)), ((), ())))
        return carry

    lax.fori_loop(0, VH * VH // 256, columns, 0)
    for e in range(4):
        source = lax.rem(y - e + 4, 4)
        for half in range(2):
            group = e * 2 + half
            at = pl.ds(pl.multiple_of(source * 2048 + half * 1024, 1024), 1024)
            total = base[:, at] + turned_ref[group * 16 : group * 16 + 16, :]
            residual[:, :, at] = total.reshape(8, 2, 1024)
            ratio = total / (pair[pl.ds(source * 2 + half, 1), :] - first - second)
            updated[:, :, at] = t_ref[:, :, at] + ratio.reshape(8, 2, 1024)


VMEM = pl.BlockSpec(memory_space=pltpu.VMEM)


def shape(*dims):
    return jax.ShapeDtypeStruct(dims, F32)


def call(kernel, name, operands, outs, scratch=(), limit=8, cost=None):
    return pl.pallas_call(
        kernel,
        in_specs=[VMEM] * len(operands),
        out_specs=[VMEM] * len(outs),
        out_shape=[shape(*dims) if isinstance(dims, tuple) else dims for dims in outs],
        scratch_shapes=[pltpu.VMEM(dims, F32) for dims in scratch],
        compiler_params=pltpu.CompilerParams(vmem_limit_bytes=limit * 1024 * 1024),
        cost_estimate=cost,
        name=name,
    )(*operands)


def load(array, part):
    return pl.pallas_call(
        lambda *refs: load_kernel(part, *refs),
        in_specs=[pl.BlockSpec(memory_space=pltpu.HBM)],
        out_specs=VMEM,
        out_shape=shape(COLS, HALF),
        scratch_shapes=[pltpu.SemaphoreType.DMA((LOADS,))],
        compiler_params=pltpu.CompilerParams(vmem_limit_bytes=1024 * 1024),
        cost_estimate=pl.CostEstimate(flops=0, bytes_accessed=8 << 20, transcendentals=0),
        name="load",
    )(array)


def shards(amplitudes, residual_in, ladder_ints, occ_energy, virt_energy, virt_order):
    own, *firsts = call(
        relayout_kernel, "relayout", [amplitudes], [(16, NP)] + [(32, RANGE)] * (2 * STREAMS)
    )
    pair_energy, turn_matrix = call(
        prepare_kernel,
        "prepare",
        [virt_order.reshape(1, NV), virt_energy.reshape(1, NV)],
        [(IRREPS, VH * VH), jax.ShapeDtypeStruct((VH * VH, VH * VH), BF16)],
        limit=16,
    )

    y_next, z_next = firsts[::2], firsts[1::2]
    arrived, loaded, pending = [[] for _ in range(STREAMS)], [], None
    partner = shift(ladder_ints, dc=1)
    for turn in range(1, 7):
        for stream in range(STREAMS):
            y_came = shift(y_next[stream], dy=1, way=1)
            z_came = shift(z_next[stream], dz=1, way=1)
            arrived[stream] += [y_came, z_came]
            if turn < 6:
                rows = len(sent_along(turn + 1)) * 16
                y_next[stream], z_next[stream] = call(
                    lambda *refs, turn=turn: round_kernel(turn, *refs),
                    "round",
                    [y_came, z_came],
                    [(rows, RANGE)] * 2,
                )
            if turn == 4 and stream == 0:
                y_next[0], pair_energy, turn_matrix = lax.optimization_barrier(
                    (y_next[0], pair_energy, turn_matrix)
                )
            if turn < 6 and stream == 0 and pending is not None:
                y_next[0], pending = lax.optimization_barrier((y_next[0], pending))
                loaded.append(pending)
            if turn < 5 and stream == STREAMS - 1:
                n = turn - 1
                source = lax.optimization_barrier(((ladder_ints, partner)[n % 2], y_came))[0]
                pending = load(source, n // 2)

    cost = pl.CostEstimate(flops=2 * 3 * ROWS * 2 * COLS * 2 * RANGE, bytes_accessed=6 << 20, transcendentals=0)
    sums = (2, 16, 16, COLS)
    total = (ROWS, 2 * COLS)
    first = []
    for stream in range(STREAMS - 1):
        held = stream * 2 * RANGE // HALF * 2
        first = list(call(
            lambda *refs, stream=stream: stream_kernel(stream, *refs),
            "stream",
            [own] + arrived[stream] + loaded[held : held + 2] + first,
            [sums],
            [total],
            limit=MULTIPLY_LIMIT,
            cost=cost,
        ))
    results = call(
        last_stream_kernel,
        "last_stream",
        [own] + arrived[STREAMS - 1] + loaded[2:] + first,
        [(4, 2, 16, COLS)] * 4 + [(2, 2, 2, 2, 8, COLS)] * 4,
        [total, sums],
        limit=MULTIPLY_LIMIT,
        cost=cost,
    )

    direct, crossed = results[:4], results[4:]
    came = [crossed[0]] + [shift(crossed[dx], dx=dx) for dx in range(1, 4)]
    direct = [direct[0]] + [shift(direct[dy], dy=-dy, way=1) for dy in range(1, 4)]
    chunk, mixed = (4, 2, 8, COLS), (12, 2, 8, COLS)
    *z_sent, home = call(
        z_pack_kernel,
        "z_pack",
        came + direct,
        [mixed if d > 4 else chunk for d in range(8)] + [(2, 4, 2, 8, COLS)],
        [(4, 2, 2, 2, 2, 8, COLS)],
    )
    z_came = [z_sent[0]] + [shift(z_sent[d], dz=d, way=1) for d in range(1, 8)]
    y_sent = call(y_pack_kernel, "y_pack", z_came, [(4, 2, 2, 8, COLS)] * 4, [(8,) + chunk])
    mirror = [y_sent[0]] + [shift(y_sent[e], dy=e) for e in range(1, 4)]
    straight = z_came[5:]
    (base,) = call(base_kernel, "base", straight + [home, residual_in], [(16, NP)], [(2, 4) + chunk])
    (swapped,) = call(swap_pack_kernel, "swap_pack", mirror, [(4, 4, 2, 8, COLS)])
    swapped = shift(swapped, dc=1)
    residual, updated = call(
        final_kernel,
        "final",
        mirror + [swapped, amplitudes, base, pair_energy, occ_energy.reshape(1, 64), turn_matrix],
        [(8, 2, NP)] * 2,
        [(128, VH * VH)] * 2,
    )
    return residual, updated


def solution(mesh):
    placed = (P("ia", "ja", None), P("ia", "ja", None), P("ja", None), P(), P(), P())
    return jax.shard_map(
        shards,
        mesh=mesh,
        in_specs=placed,
        out_specs=(P("ia", "ja", None), P("ia", "ja", None)),
        check_vma=False,
    )
```
